256 devices in a mesh: lat: 8 (over x, y_hi), lon: 32 (over z, y_lo, core).
Axes of the slice: x: 4, y: 4 (y_hi: 2, y_lo: 2; y = y_hi * 2 + y_lo), z: 8, core: 2. Of those that a mesh axis runs over, the one named last changes fastest.
Arguments:
- fields: bfloat16 [192, 128, 4096], P(None, 'lat', 'lon'), may hold values from -27.5 to 27.5
- cotangent: bfloat16 [192, 128, 4096], P(None, 'lat', 'lon'), may hold values from -6 to 6
- land_sea: int32 [128, 4096], P('lat', 'lon'), may hold values 0 or 1
- kernel: bfloat16 [192, 7, 7], replicated, may hold values from -0.875 to 0.875
- ln_gain: float32 [192], replicated, may hold values from 0.1 to 1.9
- proj_in: bfloat16 [768, 192], replicated, may hold values from -0.4375 to 0.4375
- proj_out: bfloat16 [192, 768], replicated, may hold values from -0.21875 to 0.21875
Outputs:
- updated: bfloat16 [192, 128, 4096], P(None, 'lat', 'lon')
- grad_fields: bfloat16 [192, 128, 4096], P(None, 'lat', 'lon')
- grad_kernel: float32 [192, 7, 7], replicated
- grad_gain: float32 [192], replicated
- grad_proj_in: float32 [768, 192], replicated
- grad_proj_out: float32 [192, 768], replicated
The draws below stay inside these ranges and needn't reach their ends.
All inputs are finite; a program needn't handle non-finite values. No bound on the sum of `land_sea` on one device may be relied on, other than what follows from the above.
Results may differ from the reference program's by a relative error of at most 0.007.
Values may be sent and summed in bfloat16 or wider, within the bound.
No kernel may reach another device: no remote copies, remote signals or barrier semaphores. Data moves between devices by JAX's collectives and lax.ppermute only.
A program may use at most 128 MiB of HBM per device.

```python
import math
from functools import partial
import jax
import jax.numpy as jnp
from jax import lax

CH = 192
HID = 768
NH = 128
NW = 4096


def draw_fields(key, part):
    key = jax.random.fold_in(key, 11)
    subkeys = jax.random.split(key, 3)
    log_low = math.log(0.3)
    log_high = math.log(3.0)
    channel_scale = jnp.exp(jax.random.uniform(subkeys[0], (CH, 1, 1), jnp.float32, log_low, log_high))
    cell_scale = jnp.exp(jax.random.uniform(subkeys[1], (1, NH, NW), jnp.float32, log_low, log_high))
    values = jnp.clip(jax.random.normal(subkeys[2], (CH, NH, NW), jnp.float32), -3.0, 3.0)
    return (channel_scale * cell_scale * values).astype(jnp.bfloat16)


def set_ends(values, key, low, high):
    place = [jax.random.randint(jax.random.fold_in(key, axis), (), 0, length) for axis, length in enumerate(values.shape)]
    main_axis = values.shape.index(max(values.shape))
    beside = place[:main_axis] + [(place[main_axis] + 1) % values.shape[main_axis]] + place[main_axis + 1:]
    return values.at[tuple(place)].set(low).at[tuple(beside)].set(high)


def block_levels(stream_key, shape, cuts, smallest, top_value):
    loudness, own = 1.0, jax.random.fold_in(stream_key, 6)
    for axis_at, parts in cuts:
        heights = jnp.exp(jax.random.uniform(jax.random.fold_in(own, axis_at), (parts,), jnp.float32, smallest / len(cuts), top_value / len(cuts)))
        loudness = loudness * jnp.repeat(heights, shape[axis_at] // parts).reshape([-1 if axis == axis_at else 1 for axis in range(len(shape))])
    return loudness


def gaussian(key, shape, width, reach, cuts=(), kind=jnp.bfloat16):
    loudness = block_levels(key, shape, cuts, -0.22, 0.18) if cuts else 1.0
    values = jax.random.normal(key, shape, jnp.float32) * width * loudness
    return jnp.minimum(jnp.maximum(values, -reach), reach).astype(kind)


def setup_inputs(seed: int = 0) -> dict:
    keys = jax.random.split(jax.random.key(seed), 8)
    return {
        "fields": draw_fields(jax.random.fold_in(keys[7], 71), 0),
        "cotangent": gaussian(keys[1], (CH, NH, NW), 1.0, 6.0, ((1, 8), (2, 32))),
        "land_sea": set_ends((jax.random.randint(keys[2], (NH, NW), 0, 4) < 3).astype(jnp.int32), jax.random.fold_in(keys[2], 1), 0, 1),
        "kernel": gaussian(keys[3], (CH, 7, 7), 49 ** -0.5, 0.875),
        "ln_gain": jnp.clip(1.0 + 0.18 * jax.random.normal(keys[4], (CH,), jnp.float32), 0.1, 1.9),
        "proj_in": gaussian(keys[5], (HID, CH), CH ** -0.5, 0.4375),
        "proj_out": gaussian(keys[6], (CH, HID), HID ** -0.5, 0.21875),
    }


def pad_field(source):
    widened = jnp.concatenate([source[..., -3:], source, source[..., :3]], axis=-1)
    folded = jnp.flip(widened[:, -3:, :], axis=(1, 2))
    south = jnp.zeros((source.shape[0], 3, widened.shape[2]), source.dtype)
    return jnp.concatenate([south, widened, folded], axis=1)

def shifted_sum(padded, weights):
    accum = jnp.zeros((padded.shape[0], NH, NW), padded.dtype)
    for row_off in range(7):
        for col_off in range(7):
            accum = accum + weights[:, row_off, col_off][:, None, None] * padded[:, row_off:row_off + NH, col_off:col_off + NW]
    return accum

def conv_group(items):
    field_part, weights = items
    padded = pad_field(field_part.astype(jnp.float32))
    return shifted_sum(padded, weights.astype(jnp.float32))

def back_group(items):
    field_part, weights, grad_part = items
    source = field_part.astype(jnp.float32)
    padded, pullback = jax.vjp(pad_field, source)
    weights = weights.astype(jnp.float32)
    grad_wide = grad_part.astype(jnp.float32)
    grad_pad = jnp.zeros_like(padded)
    kernel_rows = []
    for row_off in range(7):
        kernel_cols = []
        for col_off in range(7):
            grad_pad = grad_pad + weights[:, row_off, col_off][:, None, None] * jnp.pad(grad_wide, ((0, 0), (row_off, 6 - row_off), (col_off, 6 - col_off)))
            kernel_cols.append(lax.optimization_barrier(jnp.sum(grad_wide * padded[:, row_off:row_off + NH, col_off:col_off + NW], axis=(1, 2))))
        kernel_rows.append(jnp.stack(kernel_cols, axis=1))
    return (pullback(grad_pad)[0], jnp.stack(kernel_rows, axis=1))

def norm_mlp(conv_cells, field_cells, cot_cells, ocean_cells, ln_gain, proj_in, proj_out):
    center = conv_cells - lax.optimization_barrier(jnp.mean(conv_cells, axis=0, keepdims=True))
    spread = lax.rsqrt(lax.optimization_barrier(jnp.mean(center * center, axis=0, keepdims=True)) + 1e-06)
    normed = center * spread
    scaled = (normed * ln_gain[:, None]).astype(jnp.bfloat16)
    hidden = jnp.dot(proj_in, scaled, preferred_element_type=jnp.float32)
    active, pullback = jax.vjp(partial(jax.nn.gelu, approximate=True), hidden)
    active = active.astype(jnp.bfloat16)
    mixed_out = jnp.dot(proj_out, active, preferred_element_type=jnp.float32)
    ocean_float = ocean_cells.astype(jnp.float32)[None]
    result = (field_cells.astype(jnp.float32) + ocean_float * mixed_out).astype(jnp.bfloat16)
    masked_cot = cot_cells * ocean_cells.astype(jnp.bfloat16)[None]
    grad_out_w = jnp.dot(masked_cot, active.T, preferred_element_type=jnp.float32)
    grad_act = jnp.dot(proj_out.T, masked_cot, preferred_element_type=jnp.float32)
    grad_hidden = pullback(grad_act)[0].astype(jnp.bfloat16)
    grad_in_w = jnp.dot(grad_hidden, scaled.T, preferred_element_type=jnp.float32)
    grad_normed = jnp.dot(proj_in.T, grad_hidden, preferred_element_type=jnp.float32)
    grad_gain = lax.optimization_barrier(jnp.sum(grad_normed * normed, axis=1))
    grad_scaled = grad_normed * ln_gain[:, None]
    grad_conv = spread * (grad_scaled - lax.optimization_barrier(jnp.mean(grad_scaled, axis=0, keepdims=True)) - normed * lax.optimization_barrier(jnp.mean(grad_scaled * normed, axis=0, keepdims=True)))
    return (result, grad_conv.astype(jnp.bfloat16), grad_in_w, grad_out_w, grad_gain)

def reference(fields, cotangent, land_sea, kernel, ln_gain, proj_in, proj_out):
    channels = fields.shape[0]
    group_size = math.gcd(channels, 16)
    group_count = channels // group_size
    ocean_mask = land_sea.astype(jnp.bfloat16)
    masked = fields * ocean_mask[None]
    masked_groups = masked.reshape(group_count, group_size, NH, NW)
    kernel_groups = kernel.reshape(group_count, group_size, 7, 7)
    conv_out = lax.map(conv_group, (masked_groups, kernel_groups))
    all_cells = NH * NW
    block_cells = math.gcd(all_cells, 4096)
    blocks = all_cells // block_cells

    def arrange(values):
        return values.reshape(channels, blocks, block_cells).transpose(1, 0, 2)

    def step_block(totals_in, items):
        conv_b, field_b, cot_b, ocean_b = items
        result, grad_conv, grad_in, grad_out, grad_gain = norm_mlp(conv_b, field_b, cot_b, ocean_b, ln_gain, proj_in, proj_out)
        return ((totals_in[0] + grad_in, totals_in[1] + grad_out, totals_in[2] + grad_gain), (result, grad_conv))
    initial = (jnp.zeros((HID, channels), jnp.float32), jnp.zeros((channels, HID), jnp.float32), jnp.zeros((channels,), jnp.float32))
    totals, (results, grad_convs) = lax.scan(step_block, initial, (arrange(conv_out), arrange(fields), arrange(cotangent), land_sea.reshape(blocks, block_cells)))
    updated = results.transpose(1, 0, 2).reshape(channels, NH, NW)
    grad_conv_all = grad_convs.transpose(1, 0, 2).reshape(group_count, group_size, NH, NW)
    grad_masked, grad_kernel = lax.map(back_group, (masked_groups, kernel_groups, grad_conv_all))
    grad_fields = (cotangent.astype(jnp.float32) + land_sea.astype(jnp.float32)[None] * grad_masked.reshape(channels, NH, NW)).astype(jnp.bfloat16)
    factor = (NH * NW) ** (-0.5)
    return (updated, grad_fields, grad_kernel.reshape(channels, 7, 7) * factor, totals[2] * factor, totals[0] * factor, totals[1] * factor)
```

```python
from functools import partial
import numpy as np
import jax, jax.numpy as jnp
from jax import lax
from jax.experimental import pallas as pl
from jax.experimental.pallas import tpu as pltpu

CH, HID, R, Q = 192, 768, 16, 128
F, B = jnp.float32, jnp.bfloat16
C0 = 0.7978845608028654
C1 = C0 * 0.044715


def tap_onehot():
    oh = np.zeros((7, R, 32), np.float32)
    for r in range(R):
        for a in range(7):
            row = r + a
            slot = row - 3 if 3 <= row < R + 3 else (16 + row if row < 3 else row)
            oh[a, r, slot] = 1
    return oh


def toeplitz(kernel, north=None):
    oh = tap_onehot()
    if north is None:
        t = jnp.einsum("cab,ars->crbs", kernel, jnp.asarray(oh, B), preferred_element_type=F)
    else:
        up = np.zeros_like(oh); up[:, :, 19:] = oh[:, :, 19:]
        t = jnp.einsum("cab,ars->crbs", kernel, jnp.asarray(oh - up, B), preferred_element_type=F)
        t = t + jnp.einsum("cab,ars->crbs", north, jnp.asarray(up, B), preferred_element_type=F)
    return t.astype(B).reshape(CH, R, 224)


def band_mask():
    oh = tap_onehot().sum(0)
    return np.tile(oh[::-1], (1, 4)).astype(np.float32)


def front_kernel(e_ref, t_ref, f_ref, cot_ref, land_ref, gain_ref, pi_ref, pit_ref, po_ref, pot_ref, band_ref,
                 up_ref, gc_ref, w_ref,
                 im, s, mcs, u, g, grev, sc, mcb, act, gh, gacc, dks):
    CB = 8
    def conv_block(i, _):
        for j in range(CB):
            c = i * CB + j
            for b in range(7):
                im[c, b * 32:(b + 1) * 32, :] = e_ref[c, :, b:b + Q]
        for j in range(CB):
            c = i * CB + j
            s[pl.ds(c * R, R), :] = jnp.dot(t_ref[c], im[c], preferred_element_type=F)
        return 0
    lax.fori_loop(0, CH // CB, conv_block, 0)
    ocean = land_ref[...].astype(F)

    def sum_block(i, acc):
        for j in range(CB):
            acc = acc + s[pl.ds((i * CB + j) * R, R), :]
        return acc
    mean = lax.fori_loop(0, CH // CB, sum_block, jnp.zeros((R, Q), F)) * (1.0 / CH)

    def sq_block(i, acc):
        for j in range(CB):
            d = s[pl.ds((i * CB + j) * R, R), :] - mean
            acc = acc + d * d
        return acc
    var = lax.fori_loop(0, CH // CB, sq_block, jnp.zeros((R, Q), F)) * (1.0 / CH)
    rstd = lax.rsqrt(var + 1e-6)

    def norm_block(i, _):
        for j in range(CB):
            c = i * CB + j
            rows = pl.ds(c * R, R)
            s[rows, :] = (s[rows, :] - mean) * rstd
            mcs[rows, :] = cot_ref[c].astype(F) * ocean
        return 0
    lax.fori_loop(0, CH // CB, norm_block, 0)
    u[pl.ds(CH * R, R), :] = rstd
    gain = gain_ref[...]
    gacc[...] = jnp.zeros_like(gacc)

    def rows_step(p, _):
        r0 = p * 2
        cells = pl.ds(pl.multiple_of(p * 256, 256), 256)
        nrm = jnp.concatenate([s[pl.ds(r0, CH, stride=R), :], s[pl.ds(r0 + 1, CH, stride=R), :]], axis=1)
        scaled = (nrm * gain).astype(B)
        mc = jnp.concatenate([mcs[pl.ds(r0, CH, stride=R), :], mcs[pl.ds(r0 + 1, CH, stride=R), :]], axis=1).astype(B)
        sc[:, cells] = scaled
        mcb[:, cells] = mc
        mixed = jnp.zeros((CH, 256), F)
        gn = jnp.zeros((CH, 256), F)
        for h in range(3):
            hs = slice(h * 256, (h + 1) * 256)
            v = jnp.dot(pi_ref[hs, :], scaled, preferred_element_type=F)
            ga = jnp.dot(pot_ref[hs, :], mc, preferred_element_type=F)
            sq = v * v
            t = jnp.tanh(v * (C1 * sq + C0))
            half = 0.5 * t + 0.5
            a = v * half
            d = half + a * (1.0 - half) * (6.0 * C1 * sq + 2.0 * C0)
            ab = a.astype(B)
            gb = (ga * d).astype(B)
            act[hs, cells] = ab
            gh[hs, cells] = gb
            mixed = mixed + jnp.dot(po_ref[:, hs], ab, preferred_element_type=F)
            gn = gn + jnp.dot(pit_ref[:, hs], gb, preferred_element_type=F)
        rs = jnp.concatenate([u[pl.ds(CH * R + r0, 1), :], u[pl.ds(CH * R + r0 + 1, 1), :]], axis=1)
        gnn = gn * nrm
        gacc[...] += gnn[:, :Q] + gnn[:, Q:]
        gs = gn * gain
        m1 = jnp.sum(gs, axis=0, keepdims=True) * (1.0 / CH)
        m2 = jnp.sum(gnn * gain, axis=0, keepdims=True) * (1.0 / CH)
        gcv = rs * (gs - m1 - nrm * m2)
        u[pl.ds(r0, CH, stride=R), :] = mixed[:, :Q]
        u[pl.ds(r0 + 1, CH, stride=R), :] = mixed[:, Q:]
        g[pl.ds(r0, CH, stride=R), :] = gcv[:, :Q]
        g[pl.ds(r0 + 1, CH, stride=R), :] = gcv[:, Q:]
        grev[pl.ds(R - 1 - r0, CH, stride=R), :] = gcv[:, :Q]
        grev[pl.ds(R - 2 - r0, CH, stride=R), :] = gcv[:, Q:]
        return 0
    lax.fori_loop(0, R // 2, rows_step, 0)

    band = band_ref[...]
    nt = (((1,), (1,)), ((), ()))
    def out_block(i, _):
        los, his = [], []
        for j in range(CB):
            c = i * CB + j
            rows = pl.ds(c * R, R)
            up_ref[c] = (f_ref[c].astype(F) + ocean * u[rows, :]).astype(B)
            gc_ref[c] = g[rows, :].astype(B)
            dt = lax.dot_general(grev[rows, :].astype(B), im[c], nt, preferred_element_type=F)
            lo = pltpu.roll(dt[:, :Q] * band, 0, 1, stride=1, stride_axis=0)
            hi = jnp.concatenate([dt[:, Q:], jnp.zeros((R, 32), F)], axis=1)
            hi = pltpu.roll(hi * band, 0, 1, stride=1, stride_axis=0)
            los.append(jnp.sum(lo, axis=0, keepdims=True))
            his.append(jnp.sum(hi, axis=0, keepdims=True))
        dks[pl.ds(pl.multiple_of(i * CB, CB), CB), :Q] = jnp.concatenate(los, axis=0)
        dks[pl.ds(pl.multiple_of(i * CB, CB), CB), Q:] = jnp.concatenate(his, axis=0)
        return 0
    lax.fori_loop(0, CH // CB, out_block, 0)
    lane = lax.broadcasted_iota(jnp.int32, (CH, Q), 1) % 32
    def taps(x):
        own = pltpu.roll(x, Q - 12, 1)
        up = pltpu.roll(x, Q - 15, 1)
        low = pltpu.roll(x, Q - 31, 1)
        zero = jnp.zeros_like(x)
        return jnp.where(lane < 7, own, zero) + jnp.where((lane >= 4) & (lane < 7), up, zero) + jnp.where(lane < 3, low, zero)
    dk = taps(dks[:, :Q]) + pltpu.roll(taps(dks[:, Q:]), 8, 1)
    gg = jnp.sum(gacc[...], axis=1, keepdims=True)
    lane1 = lax.broadcasted_iota(jnp.int32, (CH, Q), 1)
    w_ref[pl.ds(12 * CH, CH), :] = jnp.where(lane1 == 127, gg, dk)
    w_ref[pl.ds(13 * CH, 64), :] = jnp.zeros((64, Q), F)
    for h in range(6):
        hs = slice(h * Q, (h + 1) * Q)
        w_ref[pl.ds(h * CH, CH), :] = lax.dot_general(mcb[...], act[hs, :], nt, preferred_element_type=F)
        w_ref[pl.ds((6 + h) * CH, CH), :] = lax.dot_general(sc[...], gh[hs, :], nt, preferred_element_type=F)


def front(e, t, fields, cot, land, gain, pi, po):
    vm = pl.BlockSpec(memory_space=pltpu.VMEM)
    return pl.pallas_call(
        front_kernel,
        out_shape=(jax.ShapeDtypeStruct((CH, R, Q), B), jax.ShapeDtypeStruct((CH, R, Q), B), jax.ShapeDtypeStruct((2560, Q), F)),
        in_specs=[vm] * 11, out_specs=(vm,) * 3,
        scratch_shapes=[
            pltpu.VMEM((CH, 224, Q), B), pltpu.VMEM((CH * R, Q), F), pltpu.VMEM((CH * R, Q), F),
            pltpu.VMEM((CH * R + R, Q), F), pltpu.VMEM((CH * R, Q), F), pltpu.VMEM((CH * R, Q), F),
            pltpu.VMEM((CH, R * Q), B), pltpu.VMEM((CH, R * Q), B), pltpu.VMEM((HID, R * Q), B), pltpu.VMEM((HID, R * Q), B),
            pltpu.VMEM((CH, Q), F), pltpu.VMEM((CH, 256), F),
        ],
        compiler_params=pltpu.CompilerParams(vmem_limit_bytes=56 << 20),
        name="front",
    )(e, t, fields, cot, land, gain.reshape(CH, 1), pi, pi.T, po, po.T, jnp.asarray(band_mask()))


def back_kernel(e_ref, t_ref, cot_ref, land_ref, o_ref, im):
    ocean = land_ref[...].astype(F)
    n = e_ref.shape[0]
    for c in range(n):
        for b in range(7):
            im[c, b * 32:(b + 1) * 32, :] = e_ref[c, :, b:b + Q]
    for c in range(n):
        gm = jnp.dot(t_ref[c], im[c], preferred_element_type=F)
        o_ref[c] = (cot_ref[c].astype(F) + ocean * gm).astype(B)


def back(e, t, cot, land):
    CB = 16
    return pl.pallas_call(
        back_kernel,
        grid=(CH // CB,),
        out_shape=jax.ShapeDtypeStruct((CH, R, Q), B),
        in_specs=[pl.BlockSpec((CB, 32, 134), lambda i: (i, 0, 0)), pl.BlockSpec((CB, R, 224), lambda i: (i, 0, 0)),
                  pl.BlockSpec((CB, R, Q), lambda i: (i, 0, 0)), pl.BlockSpec((R, Q), lambda i: (0, 0))],
        out_specs=pl.BlockSpec((CB, R, Q), lambda i: (i, 0, 0)),
        scratch_shapes=[pltpu.VMEM((CB, 224, Q), B)],
        compiler_params=pltpu.CompilerParams(vmem_limit_bytes=40 << 20),
        name="back",
    )(e, t, cot, land)


PLANES = ("x", "yh", "yl")
ALL = ("x", "yh", "z", "yl", "c")
LAT, LON = 8, 32


def lon_route(step):
    return [(y * LON + i, y * LON + (i + step) % LON) for y in range(LAT) for i in range(LON)]


def widen(block):
    left = lax.ppermute(block[:, :, Q - 3:], ALL, lon_route(1))
    right = lax.ppermute(block[:, :, :3], ALL, lon_route(-1))
    wide = jnp.concatenate([left, block, right], axis=2)
    low, high = wide[:, :3], wide[:, R - 3:]
    south = lax.ppermute(high, ALL, [(y * LON + i, (y + 1) * LON + i) for y in range(LAT - 1) for i in range(LON)])
    north = lax.ppermute(low, ALL, [(y * LON + i, (y - 1) * LON + i) for y in range(1, LAT) for i in range(LON)])
    top = LON * (LAT - 1)
    fold = lax.ppermute(high, ALL, [(top + i, top + LON - 1 - i) for i in range(LON)])
    mirror = jnp.asarray(np.eye(Q + 6)[::-1], B)
    fold = jnp.einsum("crq,qp->crp", fold[:, ::-1], mirror, preferred_element_type=F).astype(B)
    rest = jnp.zeros((CH, 10, Q + 6), B)
    return jnp.concatenate([wide, south, north + fold, rest], axis=1)


def exchange(value, axes, parts):
    return lax.all_to_all(jnp.broadcast_to(value[None], (parts,) + value.shape), axes, 0, 0)


def total(w):
    swap = [(i, i ^ 1) for i in range(256)]
    core = lax.axis_index("c")
    halves = w.reshape(2, 16, 80, Q)
    own = jnp.where(core == 0, halves[0], halves[1])
    other = jnp.where(core == 0, halves[1], halves[0]).astype(B)
    part = (own + lax.ppermute(other, ALL, swap).astype(F)).astype(B)
    part = lax.all_to_all(part, PLANES, 0, 0)
    part = jnp.sum(part.astype(F), axis=0).astype(B)
    part = exchange(part, ("z",), 8)
    part = (jnp.sum(part.astype(F), axis=0) * (128 * 4096) ** -0.5).astype(B)
    part = exchange(part, PLANES, 16)
    other = lax.ppermute(part, ALL, swap)
    first = jnp.where(core == 0, part, other).reshape(1280, Q)
    second = jnp.where(core == 0, other, part).reshape(1280, Q)
    return jnp.concatenate([first, second], axis=0)


def on_device(fields, cotangent, land_sea, kernel, ln_gain, proj_in, proj_out):
    lat = lax.axis_index("x") * 2 + lax.axis_index("yh")
    ocean = land_sea.astype(B)
    ext = widen(fields * ocean[None])
    updated, grad_conv, w = front(ext, toeplitz(kernel), fields, cotangent, land_sea, ln_gain, proj_in, proj_out)
    turned = jnp.flip(kernel, axis=(1, 2))
    grad_ext = widen(grad_conv)
    grad_fields = back(grad_ext, toeplitz(turned, jnp.where(lat == LAT - 1, kernel, turned)), cotangent, land_sea)
    w = total(w).astype(F)
    grad_out = w[:6 * CH].reshape(6, CH, Q).transpose(1, 0, 2).reshape(CH, HID)
    grad_in = w[6 * CH:12 * CH].reshape(6, CH, Q).transpose(0, 2, 1).reshape(HID, CH)
    tail = w[12 * CH:13 * CH]
    starts = [32 * (b % 4) + 8 * (b // 4) for b in range(7)]
    grad_kernel = jnp.stack([tail[:, i:i + 7] for i in starts], axis=2)
    return updated, grad_fields, grad_kernel, tail[:, Q - 1], grad_in, grad_out


def solution(mesh):
    fine = jax.sharding.Mesh(mesh.devices.reshape(4, 2, 8, 2, 2), ALL)
    P = jax.sharding.PartitionSpec
    lat, lon = ("x", "yh"), ("z", "yl", "c")
    block = P(None, lat, lon)
    return jax.shard_map(
        on_device,
        mesh=fine,
        in_specs=(block, block, P(lat, lon), P(), P(), P(), P()),
        out_specs=(block, block, P(), P(), P(), P()),
        check_vma=False,
    )
```

```python
import numpy as np
import jax
import jax.numpy as jnp
from jax import lax
from jax.experimental import pallas as pl
from jax.experimental.pallas import tpu as pltpu

CH, HID, R, Q = 192, 768, 16, 128
TAPS = 176
BLOCKS = 32
MSG = 3 * CH + 96
F, B = jnp.float32, jnp.bfloat16
C0 = 0.7978845608028654
C1 = C0 * 0.044715
NT = (((1,), (1,)), ((), ()))
VM = pl.BlockSpec(memory_space=pltpu.VMEM)
SM = pl.BlockSpec(memory_space=pltpu.SMEM)


def rim_base(b):
    return 112 + 8 * b if b < 2 else 128 + 8 * (b - 2)


def turn(base, shift):
    return base // 128 * 128 + (base % 128 + shift) % 128


def tables():
    inner = np.zeros((49, 256), np.float32)
    upper = np.zeros((49, 256), np.float32)
    valid = np.zeros((R, 256), np.float32)
    collect = np.zeros((256, Q), np.float32)
    for b in range(7):
        own, rim = 16 * b, rim_base(b)
        for a in range(7):
            tap, goal = a * 7 + b, 8 * a + b
            inner[tap, turn(own, a - 3)] += 1
            collect[turn(own, a + 12), goal] += 1
            if a < 3:
                inner[tap, turn(rim, a)] += 1
                collect[turn(rim, a + 15), goal] += 1
            if a > 3:
                upper[tap, turn(rim, a - 15)] += 1
                collect[turn(rim, a), goal] += 1
        for r in range(R):
            for a in range(7):
                row = r + a
                if 3 <= row < R + 3:
                    valid[r, own + row - 3] = 1
                elif row < 3:
                    valid[r, rim + row] = 1
                else:
                    valid[r, rim + row - 15] = 1
    assert (inner + upper).sum(0).max() == 1 and collect.sum(1).max() == 1
    return inner, upper, valid, collect


INNER, UPPER, VALID, COLLECT = tables()


def lanes(rows):
    return lax.broadcasted_iota(jnp.int32, (rows, Q), 1)


def shifted(own, side, step, lane):
    if step == 0:
        return own
    if step > 0:
        return pltpu.roll(jnp.where(lane < step, side, own), Q - step, 1)
    return pltpu.roll(jnp.where(lane >= Q + step, side, own), -step, 1)


def pack_sides(tile, c, held, lane):
    j = c % 16
    moved = pltpu.roll(tile, 8 * j + 3, 1)
    return moved if held is None else jnp.where(lane >= 8 * j, moved, held)


def prepare_kernel(at_ref, taps_ref, tab_ref, valid_ref, pit_ref, po_ref, gain_ref, t1_ref, t2_ref, pi_ref, pot_ref, col_ref, k1, k2):
    def spread_taps(n):
        cut = slice(n * 256, (n + 1) * 256)
        parts = [lax.dot_general(taps_ref[a], tab_ref[a, :, cut], (((0,), (0,)), ((), ())), preferred_element_type=F) for a in range(7)]
        return sum(parts[1:], parts[0])
    k1[...] = spread_taps(0)
    k2[...] = spread_taps(1)

    @pl.when(at_ref[0] != 0)
    def _():
        k2[...] = spread_taps(2)

    def block(i, _):
        rows = pl.ds(pl.multiple_of(i * 16, 16), 16)
        for src, dst in ((k1, t1_ref), (k2, t2_ref)):
            k = src[rows, :]
            for j in range(16):
                for h in range(2):
                    cut = slice(h * Q, (h + 1) * Q)
                    x = jnp.broadcast_to(k[j:j + 1, cut], (R, Q))
                    x = pltpu.roll(x, 0, 1, stride=1, stride_axis=0) * valid_ref[:, cut]
                    dst[i * 16 + j, :, cut] = x.astype(B)
        return 0
    lax.fori_loop(0, CH // 16, block, 0)
    pi_ref[...] = jnp.transpose(pit_ref[...].astype(F)).astype(B)
    pot_ref[...] = jnp.transpose(po_ref[...].astype(F)).astype(B)
    col_ref[...] = jnp.transpose(jnp.broadcast_to(gain_ref[...], (8, CH)))[:, :1]


def prepare(at, kernel, pit, po, gain):
    tab = np.concatenate([INNER + UPPER, (INNER + UPPER)[::-1], INNER[::-1] + UPPER], axis=1)
    mat = jax.ShapeDtypeStruct((CH, R, 256), B)
    return pl.pallas_call(
        prepare_kernel,
        out_shape=(mat, mat, jax.ShapeDtypeStruct((HID, CH), B), jax.ShapeDtypeStruct((HID, CH), B), jax.ShapeDtypeStruct((CH, 1), F)),
        in_specs=[SM] + [VM] * 6, out_specs=(VM,) * 5, name="prepare",
        scratch_shapes=[pltpu.VMEM((CH, 256), F)] * 2,
        compiler_params=pltpu.CompilerParams(vmem_limit_bytes=56 << 20),
        cost_estimate=pl.CostEstimate(flops=1 << 30, bytes_accessed=8 << 20, transcendentals=0),
    )(at, kernel.transpose(1, 2, 0), jnp.asarray(tab.reshape(7, 7, 768), B), jnp.asarray(VALID), pit, po, gain.reshape(1, CH))


def start_kernel(f_ref, land_ref, m_ref, side_ref, low_ref, high_ref, s):
    ocean = land_ref[...].astype(F)
    lane = lanes(R)
    def block(i, _):
        for t in range(2):
            held = None
            for j in range(16):
                c = i * 32 + t * 16 + j
                x = f_ref[c].astype(F) * ocean
                s[pl.ds(c * R, R), :] = x
                x = x.astype(B)
                m_ref[c] = x
                held = pack_sides(x, j, held, lane)
            side_ref[i * 2 + t] = held
        return 0
    lax.fori_loop(0, CH // 32, block, 0)
    for k in range(3):
        low_ref[pl.ds(k * CH, CH), :] = s[pl.ds(k, CH, stride=R), :].astype(B)
        high_ref[pl.ds(k * CH, CH), :] = s[pl.ds(R - 3 + k, CH, stride=R), :].astype(B)


def start(fields, land):
    rim = jax.ShapeDtypeStruct((3 * CH, Q), B)
    return pl.pallas_call(
        start_kernel,
        out_shape=(jax.ShapeDtypeStruct((CH, R, Q), B), jax.ShapeDtypeStruct((12, R, Q), B), rim, rim),
        in_specs=[VM] * 2, out_specs=(VM,) * 4, scratch_shapes=[pltpu.VMEM((CH * R, Q), F)], name="start",
        compiler_params=pltpu.CompilerParams(vmem_limit_bytes=56 << 20),
    )(fields, land)


def corner_kernel(left_ref, right_ref, low_ref, high_ref, *refs):
    side_ref, lo_ref, hi_ref = refs[1:4] if len(refs) > 3 else refs
    lane = lanes(R) % 8
    rows = 3 * CH
    lo_ref[:rows, :] = low_ref[...]
    hi_ref[:rows, :] = high_ref[...]
    both = [jnp.where(lane < 3, left_ref[t].astype(F), right_ref[t].astype(F)) for t in range(12)]
    for t in range(12):
        side_ref[t] = both[t].astype(B)
    for t in range(0, 12, 2):
        here = pl.ds(rows + 8 * t, 16)
        lo_ref[here, :] = jnp.concatenate([both[t][:8], both[t + 1][:8]], axis=0).astype(B)
        hi_ref[here, :] = jnp.concatenate([both[t][8:], both[t + 1][8:]], axis=0).astype(B)


def corners(left, right, low, high, *later):
    msg = jax.ShapeDtypeStruct((MSG, Q), B)
    anywhere = [pl.BlockSpec(memory_space=pl.ANY)] * len(later)
    return pl.pallas_call(
        corner_kernel,
        out_shape=(jax.ShapeDtypeStruct((12, R, Q), B), msg, msg) + tuple(jax.ShapeDtypeStruct(x.shape, x.dtype) for x in later),
        in_specs=[VM] * 4 + anywhere, out_specs=(VM,) * 3 + tuple(anywhere), name="corners",
        input_output_aliases={4: 3} if later else {},
        compiler_params=pltpu.CompilerParams(vmem_limit_bytes=8 << 20),
    )(left, right, low, high, *later)


def unpack_rims(top, south_ref, north_ref, fold_ref, mirror_ref, rim, edge):
    rim[...] = jnp.zeros_like(rim)
    rows = 3 * CH
    for k in range(3):
        rim[pl.ds(k, CH, stride=8), :] = south_ref[pl.ds(k * CH, CH), :].astype(F)
    up = lax.broadcasted_iota(jnp.int32, (8, Q), 0) >= 4

    @pl.when(top == 0)
    def _():
        for k in range(3):
            rim[pl.ds(4 + k, CH, stride=8), :] = north_ref[pl.ds(k * CH, CH), :].astype(F)
        for t in range(0, 12, 2):
            n, z = north_ref[pl.ds(rows + 8 * t, 16), :].astype(F), south_ref[pl.ds(rows + 8 * t, 16), :].astype(F)
            for h in range(2):
                cut = slice(8 * h, 8 * h + 8)
                edge[t + h] = jnp.where(up, pltpu.roll(n[cut], 4, 0), pltpu.roll(z[cut], 3, 0))

    @pl.when(top != 0)
    def _():
        for k in range(3):
            plane = jnp.dot(fold_ref[pl.ds(k * CH, CH), :], mirror_ref[:, :Q], preferred_element_type=F)
            rim[pl.ds(6 - k, CH, stride=8), :] = plane
        for t in range(0, 12, 2):
            n = jnp.dot(fold_ref[pl.ds(rows + 8 * t, 16), :], mirror_ref[:, Q:], preferred_element_type=F)
            z = south_ref[pl.ds(rows + 8 * t, 16), :].astype(F)
            for h in range(2):
                x = n[8 * h:8 * h + 8]
                flip = jnp.concatenate([x[:4], x[7:8], x[6:7], x[5:6], x[4:5]], axis=0)
                edge[t + h] = jnp.where(up, flip, pltpu.roll(z[8 * h:8 * h + 8], 3, 0))


def mirrors():
    cols = np.eye(Q, dtype=np.float32)[::-1]
    ends = np.zeros((Q, Q), np.float32)
    for g in range(16):
        for k in range(6):
            ends[8 * g + k, 8 * g + 5 - k] = 1
    return jnp.asarray(np.concatenate([cols, ends], axis=1), B)


def operand(c, j, own, side, rim, edge, out):
    back = (Q - (8 * j + 3)) % Q
    beside = pltpu.roll(side, back, 1)
    lane = lanes(R)
    for b in range(7):
        out[b * R:(b + 1) * R, :] = shifted(own, beside, b - 3, lane)
    beside = pltpu.roll(edge, back, 1)
    lane = lanes(8)
    rims = [shifted(rim, beside, b - 3, lane) for b in range(7)] + [jnp.zeros((8, Q), F)]
    for b in range(0, 8, 2):
        out[112 + 8 * b:128 + 8 * b, :] = jnp.concatenate(rims[b:b + 2], axis=0).astype(B)


def front_kernel(at_ref, m_ref, side_ref, south_ref, north_ref, fold_ref, t_ref, f_ref, cot_ref, land_ref, gain_ref,
                 pi_ref, pit_ref, po_ref, pot_ref, mirror_ref,
                 up_ref, gc_ref, grev_ref, gside_ref, low_ref, high_ref, gacc, wall,
                 im, rim, edge, s, mcs, u, g, grev, sc, mcb, act, gh):
    unpack_rims(at_ref[0], south_ref, north_ref, fold_ref, mirror_ref, rim, edge)

    def conv_block(i, _):
        for j in range(BLOCKS):
            c = i * BLOCKS + j
            t = i * (BLOCKS // 16) + j // 16
            operand(c, j % 16, m_ref[c], side_ref[t], rim[pl.ds(pl.multiple_of(c * 8, 8), 8), :], edge[t], im.at[c])
        for j in range(BLOCKS):
            c = i * BLOCKS + j
            s[pl.ds(pl.multiple_of(c * R, R), R), :] = jnp.dot(t_ref[c][:, :TAPS], im[c], preferred_element_type=F)
        return 0
    lax.fori_loop(0, CH // BLOCKS, conv_block, 0)
    ocean = land_ref[...].astype(F)

    def sum_block(i, acc):
        for j in range(BLOCKS):
            acc = acc + s[pl.ds(pl.multiple_of((i * BLOCKS + j) * R, R), R), :]
        return acc
    mean = lax.fori_loop(0, CH // BLOCKS, sum_block, jnp.zeros((R, Q), F)) * (1.0 / CH)

    def sq_block(i, acc):
        for j in range(BLOCKS):
            d = s[pl.ds(pl.multiple_of((i * BLOCKS + j) * R, R), R), :] - mean
            acc = acc + d * d
        return acc
    var = lax.fori_loop(0, CH // BLOCKS, sq_block, jnp.zeros((R, Q), F)) * (1.0 / CH)
    rstd = lax.rsqrt(var + 1e-6)

    def norm_block(i, _):
        for j in range(BLOCKS):
            c = i * BLOCKS + j
            rows = pl.ds(pl.multiple_of(c * R, R), R)
            s[rows, :] = (s[rows, :] - mean) * rstd
            mcs[rows, :] = cot_ref[c].astype(F) * ocean
        return 0
    lax.fori_loop(0, CH // BLOCKS, norm_block, 0)
    u[pl.ds(CH * R, R), :] = rstd
    gain = gain_ref[...]
    gacc[...] = jnp.zeros_like(gacc)

    def rows_step(p, _):
        r0 = p * 2
        cells = pl.ds(pl.multiple_of(p * 256, 256), 256)
        nrm = jnp.concatenate([s[pl.ds(r0, CH, stride=R), :], s[pl.ds(r0 + 1, CH, stride=R), :]], axis=1)
        scaled = (nrm * gain).astype(B)
        mc = jnp.concatenate([mcs[pl.ds(r0, CH, stride=R), :], mcs[pl.ds(r0 + 1, CH, stride=R), :]], axis=1).astype(B)
        sc[:, cells] = scaled
        mcb[:, cells] = mc
        mixed = jnp.zeros((CH, 256), F)
        gn = jnp.zeros((CH, 256), F)
        hidden = jnp.dot(pi_ref[...], scaled, preferred_element_type=F)
        grad_act = jnp.dot(pot_ref[...], mc, preferred_element_type=F)
        for h in range(3):
            hs = slice(h * 256, (h + 1) * 256)
            v = hidden[hs]
            ga = grad_act[hs]
            sq = v * v
            t = jnp.tanh(v * (C1 * sq + C0))
            half = 0.5 * t + 0.5
            a = v * half
            d = half + a * (1.0 - half) * (6.0 * C1 * sq + 2.0 * C0)
            ab = a.astype(B)
            gb = (ga * d).astype(B)
            act[hs, cells] = ab
            gh[hs, cells] = gb
            mixed = mixed + jnp.dot(po_ref[:, hs], ab, preferred_element_type=F)
            gn = gn + jnp.dot(pit_ref[:, hs], gb, preferred_element_type=F)
        rs = jnp.concatenate([u[pl.ds(CH * R + r0, 1), :], u[pl.ds(CH * R + r0 + 1, 1), :]], axis=1)
        gnn = gn * nrm
        gacc[...] += gnn[:, :Q] + gnn[:, Q:]
        gs = gn * gain
        m1 = jnp.sum(gs, axis=0, keepdims=True) * (1.0 / CH)
        m2 = jnp.sum(gnn * gain, axis=0, keepdims=True) * (1.0 / CH)
        gcv = rs * (gs - m1 - nrm * m2)
        for h in range(2):
            cut = slice(h * Q, (h + 1) * Q)
            u[pl.ds(r0 + h, CH, stride=R), :] = mixed[:, cut]
            g[pl.ds(r0 + h, CH, stride=R), :] = gcv[:, cut]
            grev[pl.ds(R - 1 - r0 - h, CH, stride=R), :] = gcv[:, cut]
        return 0
    lax.fori_loop(0, R // 2, rows_step, 0)

    lane = lanes(R)

    def out_block(i, _):
        held = None
        for j in range(BLOCKS):
            c = i * BLOCKS + j
            rows = pl.ds(pl.multiple_of(c * R, R), R)
            up_ref[c] = (f_ref[c].astype(F) + ocean * u[rows, :]).astype(B)
            gb = g[rows, :].astype(B)
            gc_ref[c] = gb
            grev_ref[c] = grev[rows, :].astype(B)
            held = pack_sides(gb, j % 16, None if j % 16 == 0 else held, lane)
            if j % 16 == 15:
                gside_ref[i * (BLOCKS // 16) + j // 16] = held
        return 0
    lax.fori_loop(0, CH // BLOCKS, out_block, 0)
    for k in range(3):
        low_ref[pl.ds(k * CH, CH), :] = g[pl.ds(k, CH, stride=R), :].astype(B)
        high_ref[pl.ds(k * CH, CH), :] = g[pl.ds(R - 3 + k, CH, stride=R), :].astype(B)
    wall[pl.ds(12 * CH, 256), :] = jnp.zeros((256, Q), B)
    for h in range(6):
        hs = slice(h * Q, (h + 1) * Q)
        wall[pl.ds(h * CH, CH), :] = lax.dot_general(mcb[...], act[hs, :], NT, preferred_element_type=F).astype(B)
        wall[pl.ds((6 + h) * CH, CH), :] = lax.dot_general(sc[...], gh[hs, :], NT, preferred_element_type=F).astype(B)


def front(at, masked, side, south, north, fold, t, fields, cot, land, gain, pi, pit, po, pot):
    block, rim = jax.ShapeDtypeStruct((CH, R, Q), B), jax.ShapeDtypeStruct((3 * CH, Q), B)
    plane = pltpu.VMEM((CH * R, Q), F)
    return pl.pallas_call(
        front_kernel,
        out_shape=(block, block, block, jax.ShapeDtypeStruct((12, R, Q), B), rim, rim, jax.ShapeDtypeStruct((CH, Q), F),
                   jax.ShapeDtypeStruct((2560, Q), B)),
        in_specs=[SM] + [VM] * 15, out_specs=(VM,) * 8,
        scratch_shapes=[
            pltpu.VMEM((CH, TAPS, Q), B), pltpu.VMEM((CH * 8, Q), F), pltpu.VMEM((12, 8, Q), F),
            plane, plane, pltpu.VMEM((CH * R + R, Q), F), plane, plane,
            pltpu.VMEM((CH, R * Q), B), pltpu.VMEM((CH, R * Q), B), pltpu.VMEM((HID, R * Q), B), pltpu.VMEM((HID, R * Q), B),
        ],
        compiler_params=pltpu.CompilerParams(vmem_limit_bytes=40 << 20),
        cost_estimate=pl.CostEstimate(flops=6 << 30, bytes_accessed=12 << 20, transcendentals=3 << 20),
        name="front",
    )(at, masked, side, south, north, fold, t, fields, cot, land, gain, pi, pit, po, pot, mirrors())


def tap_kernel(at_ref, m_ref, side_ref, south_ref, north_ref, fold_ref, grev_ref, gacc_ref, mirror_ref, valid_ref, collect_ref, w_ref,
               o_ref, im, rim, edge, dks):
    unpack_rims(at_ref[0], south_ref, north_ref, fold_ref, mirror_ref, rim, edge)

    def block(i, _):
        sums = [[], []]
        for j in range(BLOCKS):
            c = i * BLOCKS + j
            t = i * (BLOCKS // 16) + j // 16
            operand(c, j % 16, m_ref[c], side_ref[t], rim[pl.ds(pl.multiple_of(c * 8, 8), 8), :], edge[t], im.at[j])
        for j in range(BLOCKS):
            dt = lax.dot_general(grev_ref[i * BLOCKS + j], im[j], NT, preferred_element_type=F)
            dt = [dt[:, :Q], jnp.concatenate([dt[:, Q:], jnp.zeros((R, 256 - TAPS), F)], axis=1)]
            for h in range(2):
                x = pltpu.roll(dt[h] * valid_ref[:, h * Q:(h + 1) * Q], 0, 1, stride=1, stride_axis=0)
                sums[h].append(jnp.sum(x, axis=0, keepdims=True))
        for h in range(2):
            dks[pl.ds(pl.multiple_of(i * BLOCKS, BLOCKS), BLOCKS), h * Q:(h + 1) * Q] = jnp.concatenate(sums[h], axis=0)
        return 0
    lax.fori_loop(0, CH // BLOCKS, block, 0)
    taps = jnp.dot(dks[...], collect_ref[...], preferred_element_type=F, precision=lax.Precision.HIGHEST)
    gg = jnp.sum(gacc_ref[...], axis=1, keepdims=True)
    o_ref[:CH, :] = jnp.where(lanes(CH) == Q - 1, gg, taps).astype(B)
    o_ref[CH:, :] = jnp.zeros((256 - CH, Q), B)


def taps(at, masked, rims, grev, gacc, w):
    return pl.pallas_call(
        tap_kernel,
        grid=(1,),
        out_shape=jax.ShapeDtypeStruct(w.shape, B),
        in_specs=[SM] + [VM] * 10 + [pl.BlockSpec(memory_space=pl.ANY)],
        out_specs=pl.BlockSpec((256, Q), lambda i: (9, 0)),
        scratch_shapes=[pltpu.VMEM((BLOCKS, TAPS, Q), B), pltpu.VMEM((CH * 8, Q), F), pltpu.VMEM((12, 8, Q), F), pltpu.VMEM((CH, 256), F)],
        compiler_params=pltpu.CompilerParams(vmem_limit_bytes=40 << 20),
        cost_estimate=pl.CostEstimate(flops=2 << 30, bytes_accessed=8 << 20, transcendentals=0),
        input_output_aliases={11: 0},
        name="taps",
    )(at, masked, *rims, grev, gacc, mirrors(), jnp.asarray(VALID[::-1].copy()), jnp.asarray(COLLECT), w)


def back_kernel(first, at_ref, m_ref, side_ref, south_ref, north_ref, fold_ref, t_ref, cot_ref, land_ref, mirror_ref, after_ref, *refs):
    o_ref, im, rim, edge = refs[-4:]
    i = pl.program_id(0)

    @pl.when(i == 0)
    def _():
        unpack_rims(at_ref[0], south_ref, north_ref, fold_ref, mirror_ref, rim, edge)
    ocean = land_ref[...].astype(F)
    for j in range(BLOCKS):
        c = (first + i) * BLOCKS + j
        t = (first + i) * (BLOCKS // 16) + j // 16
        operand(c, j % 16, m_ref[j], side_ref[t], rim[pl.ds(pl.multiple_of(c * 8, 8), 8), :], edge[t], im.at[j])
    for j in range(BLOCKS):
        gm = jnp.dot(t_ref[j][:, :TAPS], im[j], preferred_element_type=F)
        o_ref[j] = (cot_ref[j].astype(F) + ocean * gm).astype(B)


def back(at, grad, rims, t, cot, land, after, first, count, begun=None):
    some = lambda *shape: pl.BlockSpec((BLOCKS,) + shape, lambda i: (first + i, 0, 0))
    anywhere = pl.BlockSpec(memory_space=pl.ANY)
    extra = [] if begun is None else [begun]
    return pl.pallas_call(
        lambda *refs: back_kernel(first, *refs),
        grid=(count,),
        out_shape=jax.ShapeDtypeStruct((CH, R, Q), B),
        in_specs=[SM, some(R, Q), VM, VM, VM, VM, some(R, 256), some(R, Q), VM, VM, anywhere] + [anywhere] * len(extra),
        out_specs=some(R, Q),
        scratch_shapes=[pltpu.VMEM((BLOCKS, TAPS, Q), B), pltpu.VMEM((CH * 8, Q), F), pltpu.VMEM((12, 8, Q), F)],
        compiler_params=pltpu.CompilerParams(vmem_limit_bytes=56 << 20),
        cost_estimate=pl.CostEstimate(flops=1 << 30, bytes_accessed=8 << 20, transcendentals=0),
        input_output_aliases={11: 0} if extra else {},
        name="back",
    )(at, grad, *rims, t, cot, land, mirrors(), after, *extra)


def spread_kernel(x_ref, *refs):
    o_ref = refs[-1]
    total = x_ref[0].astype(F)
    for k in range(1, x_ref.shape[0]):
        total = total + x_ref[k].astype(F)
    total = total.astype(B)
    for k in range(o_ref.shape[0]):
        o_ref[k] = total


def spread(x, copies, *after):
    return pl.pallas_call(
        spread_kernel, out_shape=jax.ShapeDtypeStruct((copies,) + x.shape[1:], B),
        in_specs=[VM] + [pl.BlockSpec(memory_space=pl.ANY)] * len(after), out_specs=VM, name="spread",
        compiler_params=pltpu.CompilerParams(vmem_limit_bytes=8 << 20),
    )(x, *after)


def along(i, bits):
    code = (i ^ (i >> 1)) ^ bits
    return code ^ (code >> 1)


def finish_kernel(at_ref, a_ref, b_ref, after_ref, out_ref, in_ref, kern_ref, gain_ref, wall):
    x, y, c = at_ref[1], at_ref[2], at_ref[3]
    for k in range(32):
        src = (a_ref, b_ref)[k // 16]
        chunk = along(x, k % 4) * 8 + along(y, k // 4 % 4) * 2 + (c ^ (k // 16))
        wall[pl.ds(pl.multiple_of(chunk * 80, 80), 80), :] = src[pl.ds(k % 16 * 80, 80), :]
    scale = (128 * 4096) ** -0.5
    for h in range(6):
        hs = slice(h * Q, (h + 1) * Q)
        out_ref[:, hs] = wall[pl.ds(h * CH, CH), :].astype(F) * scale
        in_ref[:, hs] = wall[pl.ds((6 + h) * CH, CH), :].astype(F) * scale
    tail = jnp.transpose(wall[pl.ds(12 * CH, CH), :].astype(F) * scale)
    for a in range(7):
        kern_ref[a] = tail[8 * a:8 * a + 7, :]
    gain_ref[...] = tail[Q - 1:, :]


def finish(at, first, second, after):
    shapes = ((CH, HID), (CH, HID), (7, 7, CH), (1, CH))
    return pl.pallas_call(
        finish_kernel,
        out_shape=tuple(jax.ShapeDtypeStruct(x, F) for x in shapes),
        in_specs=[SM, VM, VM, pl.BlockSpec(memory_space=pl.ANY)], out_specs=(VM,) * 4, name="finish",
        scratch_shapes=[pltpu.VMEM((2560, Q), B)],
        compiler_params=pltpu.CompilerParams(vmem_limit_bytes=16 << 20),
    )(at, first, second, after)


ALL = ("x", "yh", "z", "yl", "c")
LAT, LON = 8, 32
PLANE = ("x", "yh", "yl", "c")


def lon_route(step):
    return [(y * LON + i, y * LON + (i + step) % LON) for y in range(LAT) for i in range(LON)]


def rims(side, low, high, *later):
    left = lax.ppermute(side, ALL, lon_route(1))
    right = lax.ppermute(side, ALL, lon_route(-1))
    side, low, high, *later = corners(left, right, low, high, *later)
    top = LON * (LAT - 1)
    fold = lax.ppermute(high, ALL, [(top + i, top + LON - 1 - i) for i in range(LON)])
    south = lax.ppermute(high, ALL, [(y * LON + i, (y + 1) * LON + i) for y in range(LAT - 1) for i in range(LON)])
    north = lax.ppermute(low, ALL, [(y * LON + i, (y - 1) * LON + i) for y in range(1, LAT) for i in range(LON)])
    return (side, south, north, fold), *later


def swap_route(bx=0, by=0, bc=0):
    def flat(x, y, z, c):
        return ((x * 2 + y // 2) * 8 + z) * 4 + (y % 2) * 2 + c
    return [
        (flat(x, y, z, c), flat(along(x, bx), along(y, by), z, c ^ bc))
        for x in range(4) for y in range(4) for z in range(8) for c in range(2)
    ]


def on_device(fields, cotangent, land_sea, kernel, ln_gain, proj_in, proj_out):
    x, y, c = lax.axis_index("x"), lax.axis_index("yh") * 2 + lax.axis_index("yl"), lax.axis_index("c")
    is_top = x * 2 + lax.axis_index("yh") == LAT - 1
    at = jnp.stack([is_top.astype(jnp.int32), x, y, c]).astype(jnp.int32)
    masked, side, low, high = start(fields, land_sea)
    one, two, pi, pot, gain = prepare(at, kernel, proj_in.T, proj_out, ln_gain)
    ends, one = rims(side, low, high, one)
    updated, grad, reverse, side, low, high, gacc, w = front(
        at, masked, *ends, one, fields, cotangent, land_sea, gain, pi, proj_in.T, proj_out, pot)
    w = taps(at, masked, ends, reverse, gacc, w)
    ends, w = rims(side, low, high, w)
    w = spread(lax.all_to_all(w.reshape(32, 80, Q), PLANE, 0, 0), 8, *ends)
    grad_fields = back(at, grad, ends, two, cotangent, land_sea, w, 0, 6)
    w = spread(lax.all_to_all(w, "z", 0, 0), 1, grad_fields)[0]
    w = jnp.concatenate([w] + [lax.ppermute(w, ALL, swap_route(bx=k)) for k in (1, 2, 3)])
    w = jnp.concatenate([w] + [lax.ppermute(w, ALL, swap_route(by=k)) for k in (1, 2, 3)])
    grad_out, grad_in, grad_kernel, grad_gain = finish(at, w, lax.ppermute(w, ALL, swap_route(bc=1)), grad_fields)
    return updated, grad_fields, grad_kernel.transpose(2, 0, 1), grad_gain.reshape(CH), grad_in.T, grad_out


def solution(mesh):
    fine = jax.sharding.Mesh(mesh.devices.reshape(4, 2, 8, 2, 2), ALL)
    P = jax.sharding.PartitionSpec
    lat, lon = ("x", "yh"), ("z", "yl", "c")
    block = P(None, lat, lon)
    return jax.shard_map(
        on_device,
        mesh=fine,
        in_specs=(block, block, P(lat, lon), P(), P(), P(), P()),
        out_specs=(block, block, P(), P(), P(), P()),
        check_vma=False,
    )
```

```python
import numpy as np
import jax
import jax.numpy as jnp
from jax import lax
from jax.experimental import pallas as pl
from jax.experimental.pallas import tpu as pltpu

CH, HID, R, Q = 192, 768, 16, 128
TAPS = 176
BLOCKS = 32
MSG = 3 * CH + 96
F, B = jnp.float32, jnp.bfloat16
C0 = 0.7978845608028654
C1 = C0 * 0.044715
NT = (((1,), (1,)), ((), ()))
VM = pl.BlockSpec(memory_space=pltpu.VMEM)
SM = pl.BlockSpec(memory_space=pltpu.SMEM)
ANY = pl.BlockSpec(memory_space=pl.ANY)
HBM = pl.BlockSpec(memory_space=pltpu.HBM)


def rim_base(b):
    return 112 + 8 * b if b < 2 else 128 + 8 * (b - 2)


def turn(base, shift):
    return base // 128 * 128 + (base % 128 + shift) % 128


def tables():
    inner = np.zeros((49, 256), np.float32)
    upper = np.zeros((49, 256), np.float32)
    valid = np.zeros((R, 256), np.float32)
    collect = np.zeros((256, Q), np.float32)
    for b in range(7):
        own, rim = 16 * b, rim_base(b)
        for a in range(7):
            tap, goal = a * 7 + b, 8 * a + b
            inner[tap, turn(own, a - 3)] += 1
            collect[turn(own, a + 12), goal] += 1
            if a < 3:
                inner[tap, turn(rim, a)] += 1
                collect[turn(rim, a + 15), goal] += 1
            if a > 3:
                upper[tap, turn(rim, a - 15)] += 1
                collect[turn(rim, a), goal] += 1
        for r in range(R):
            for a in range(7):
                row = r + a
                if 3 <= row < R + 3:
                    valid[r, own + row - 3] = 1
                elif row < 3:
                    valid[r, rim + row] = 1
                else:
                    valid[r, rim + row - 15] = 1
    assert (inner + upper).sum(0).max() == 1 and collect.sum(1).max() == 1
    return inner, upper, valid, collect


INNER, UPPER, VALID, COLLECT = tables()


def lanes(rows):
    return lax.broadcasted_iota(jnp.int32, (rows, Q), 1)


def shifted(own, side, step, lane):
    if step == 0:
        return own
    if step > 0:
        return pltpu.roll(jnp.where(lane < step, side, own), Q - step, 1)
    return pltpu.roll(jnp.where(lane >= Q + step, side, own), -step, 1)


def pack_sides(tile, c, held, lane):
    j = c % 16
    moved = pltpu.roll(tile, 8 * j + 3, 1)
    return moved if held is None else jnp.where(lane >= 8 * j, moved, held)


def spread_taps(taps_ref, tab_ref, n):
    cut = slice(n * 256, (n + 1) * 256)
    parts = [lax.dot_general(taps_ref[a], tab_ref[a, :, cut], (((0,), (0,)), ((), ())), preferred_element_type=F) for a in range(7)]
    return sum(parts[1:], parts[0])


def fill_matrices(k_ref, valid_ref, out_ref):
    def block(i, _):
        k = k_ref[pl.ds(pl.multiple_of(i * 16, 16), 16), :]
        for j in range(16):
            for h in range(2):
                cut = slice(h * Q, (h + 1) * Q)
                x = jnp.broadcast_to(k[j:j + 1, cut], (R, Q))
                x = pltpu.roll(x, 0, 1, stride=1, stride_axis=0) * valid_ref[:, cut]
                out_ref[i * 16 + j, :, cut] = x.astype(B)
        return 0
    lax.fori_loop(0, CH // 16, block, 0)


def forward_kernel(taps_ref, tab_ref, valid_ref, gain_ref, t_ref, col_ref, k):
    k[...] = spread_taps(taps_ref, tab_ref, 0)
    fill_matrices(k, valid_ref, t_ref)
    col_ref[...] = jnp.transpose(jnp.broadcast_to(gain_ref[...], (8, CH)))[:, :1]


def backward_kernel(at_ref, taps_ref, tab_ref, valid_ref, pit_ref, po_ref, t_ref, pi_ref, pot_ref, k):
    k[...] = spread_taps(taps_ref, tab_ref, 0)

    @pl.when(at_ref[0] != 0)
    def _():
        k[...] = spread_taps(taps_ref, tab_ref, 1)
    fill_matrices(k, valid_ref, t_ref)
    pi_ref[...] = jnp.transpose(pit_ref[...].astype(F)).astype(B)
    pot_ref[...] = jnp.transpose(po_ref[...].astype(F)).astype(B)


def forward_matrices(kernel, gain):
    return pl.pallas_call(
        forward_kernel,
        out_shape=(jax.ShapeDtypeStruct((CH, R, 256), B), jax.ShapeDtypeStruct((CH, 1), F)),
        in_specs=[VM] * 4, out_specs=(VM,) * 2, name="forward_matrices",
        scratch_shapes=[pltpu.VMEM((CH, 256), F)],
        compiler_params=pltpu.CompilerParams(vmem_limit_bytes=56 << 20),
        cost_estimate=pl.CostEstimate(flops=1 << 30, bytes_accessed=8 << 20, transcendentals=0),
    )(kernel.transpose(1, 2, 0), jnp.asarray((INNER + UPPER).reshape(7, 7, 256), B), jnp.asarray(VALID), gain.reshape(1, CH))


def backward_matrices(at, kernel, pit, po):
    tab = np.concatenate([(INNER + UPPER)[::-1], INNER[::-1] + UPPER], axis=1)
    turned = jax.ShapeDtypeStruct((HID, CH), B)
    return pl.pallas_call(
        backward_kernel,
        out_shape=(jax.ShapeDtypeStruct((CH, R, 256), B), turned, turned),
        in_specs=[SM] + [VM] * 5, out_specs=(VM,) * 3, name="backward_matrices",
        scratch_shapes=[pltpu.VMEM((CH, 256), F)],
        compiler_params=pltpu.CompilerParams(vmem_limit_bytes=56 << 20),
        cost_estimate=pl.CostEstimate(flops=1 << 30, bytes_accessed=8 << 20, transcendentals=0),
    )(at, kernel.transpose(1, 2, 0), jnp.asarray(tab.reshape(7, 7, 512), B), jnp.asarray(VALID), pit, po)


def start_kernel(f_ref, land_ref, m_ref, side_ref, low_ref, high_ref, s):
    ocean = land_ref[...].astype(F)
    lane = lanes(R)
    def block(i, _):
        for t in range(2):
            held = None
            for j in range(16):
                c = i * 32 + t * 16 + j
                x = f_ref[c].astype(F) * ocean
                s[pl.ds(c * R, R), :] = x
                x = x.astype(B)
                m_ref[c] = x
                held = pack_sides(x, j, held, lane)
            side_ref[i * 2 + t] = held
        return 0
    lax.fori_loop(0, CH // 32, block, 0)
    for k in range(3):
        low_ref[pl.ds(k * CH, CH), :] = s[pl.ds(k, CH, stride=R), :].astype(B)
        high_ref[pl.ds(k * CH, CH), :] = s[pl.ds(R - 3 + k, CH, stride=R), :].astype(B)


def start(fields, land):
    rim = jax.ShapeDtypeStruct((3 * CH, Q), B)
    return pl.pallas_call(
        start_kernel,
        out_shape=(jax.ShapeDtypeStruct((CH, R, Q), B), jax.ShapeDtypeStruct((12, R, Q), B), rim, rim),
        in_specs=[VM] * 2, out_specs=(VM,) * 4, scratch_shapes=[pltpu.VMEM((CH * R, Q), F)], name="start",
        compiler_params=pltpu.CompilerParams(vmem_limit_bytes=56 << 20),
    )(fields, land)


def corner_kernel(left_ref, right_ref, low_ref, high_ref, *refs):
    side_ref, lo_ref, hi_ref = refs[-3:]
    lane = lanes(R) % 8
    rows = 3 * CH
    lo_ref[:rows, :] = low_ref[...]
    hi_ref[:rows, :] = high_ref[...]
    both = [jnp.where(lane < 3, left_ref[t].astype(F), right_ref[t].astype(F)) for t in range(12)]
    for t in range(12):
        side_ref[t] = both[t].astype(B)
    for t in range(0, 12, 2):
        here = pl.ds(rows + 8 * t, 16)
        lo_ref[here, :] = jnp.concatenate([both[t][:8], both[t + 1][:8]], axis=0).astype(B)
        hi_ref[here, :] = jnp.concatenate([both[t][8:], both[t + 1][8:]], axis=0).astype(B)


def corners(left, right, low, high, after):
    msg = jax.ShapeDtypeStruct((MSG, Q), B)
    return pl.pallas_call(
        corner_kernel, out_shape=(jax.ShapeDtypeStruct((12, R, Q), B), msg, msg),
        in_specs=[VM] * 4 + [HBM], out_specs=(VM,) * 3, name="corners",
        compiler_params=pltpu.CompilerParams(vmem_limit_bytes=8 << 20),
    )(left, right, low, high, after)


def unpack_rims(top, south_ref, north_ref, fold_ref, mirror_ref, rim, edge):
    rim[...] = jnp.zeros_like(rim)
    rows = 3 * CH
    for k in range(3):
        rim[pl.ds(k, CH, stride=8), :] = south_ref[pl.ds(k * CH, CH), :].astype(F)
    up = lax.broadcasted_iota(jnp.int32, (8, Q), 0) >= 4

    @pl.when(top == 0)
    def _():
        for k in range(3):
            rim[pl.ds(4 + k, CH, stride=8), :] = north_ref[pl.ds(k * CH, CH), :].astype(F)
        for t in range(0, 12, 2):
            n, z = north_ref[pl.ds(rows + 8 * t, 16), :].astype(F), south_ref[pl.ds(rows + 8 * t, 16), :].astype(F)
            for h in range(2):
                cut = slice(8 * h, 8 * h + 8)
                edge[t + h] = jnp.where(up, pltpu.roll(n[cut], 4, 0), pltpu.roll(z[cut], 3, 0))

    @pl.when(top != 0)
    def _():
        for k in range(3):
            plane = jnp.dot(fold_ref[pl.ds(k * CH, CH), :], mirror_ref[:, :Q], preferred_element_type=F)
            rim[pl.ds(6 - k, CH, stride=8), :] = plane
        for t in range(0, 12, 2):
            n = jnp.dot(fold_ref[pl.ds(rows + 8 * t, 16), :], mirror_ref[:, Q:], preferred_element_type=F)
            z = south_ref[pl.ds(rows + 8 * t, 16), :].astype(F)
            for h in range(2):
                x = n[8 * h:8 * h + 8]
                flip = jnp.concatenate([x[:4], x[7:8], x[6:7], x[5:6], x[4:5]], axis=0)
                edge[t + h] = jnp.where(up, flip, pltpu.roll(z[8 * h:8 * h + 8], 3, 0))


def mirrors():
    cols = np.eye(Q, dtype=np.float32)[::-1]
    ends = np.zeros((Q, Q), np.float32)
    for g in range(16):
        for k in range(6):
            ends[8 * g + k, 8 * g + 5 - k] = 1
    return jnp.asarray(np.concatenate([cols, ends], axis=1), B)


def operand(c, j, own, side, rim, edge, out):
    back = (Q - (8 * j + 3)) % Q
    beside = pltpu.roll(side, back, 1)
    lane = lanes(R)
    for b in range(7):
        out[b * R:(b + 1) * R, :] = shifted(own, beside, b - 3, lane)
    beside = pltpu.roll(edge, back, 1)
    lane = lanes(8)
    rims = [shifted(rim, beside, b - 3, lane) for b in range(7)] + [jnp.zeros((8, Q), F)]
    for b in range(0, 8, 2):
        out[112 + 8 * b:128 + 8 * b, :] = jnp.concatenate(rims[b:b + 2], axis=0).astype(B)


def front_kernel(at_ref, m_hbm, side_ref, south_ref, north_ref, fold_ref, t_hbm, f_hbm, cot_hbm, land_ref, gain_ref,
                 pi_hbm, pit_hbm, po_hbm, pot_hbm, mirror_ref, after_ref,
                 up_hbm, gc_hbm, grev_hbm, gside_ref, low_ref, high_ref, gacc, wall, kept_ref,
                 im, rim, edge, s, mcs, u, g, grev, sc, mcb, act, gh, kept_sem,
                 m_ref, t_ref, f_ref, cot_ref, pi_ref, pit_ref, po_ref, pot_ref, m_sem, t_sem, sem,
                 up_ref, gc_ref, grev_ref, out_sem):
    def keep(i):
        here = pl.ds(i * BLOCKS, BLOCKS)
        return pltpu.make_async_copy(im.at[here], kept_ref.at[here], kept_sem.at[i])

    def fetch(i):
        here = pl.ds(i * BLOCKS, BLOCKS)
        return (pltpu.make_async_copy(m_hbm.at[here], m_ref.at[here], m_sem.at[i]),
                pltpu.make_async_copy(t_hbm.at[here], t_ref.at[here], t_sem.at[i]))
    def send(i):
        here = pl.ds(i * BLOCKS, BLOCKS)
        pairs = ((up_ref, up_hbm), (gc_ref, gc_hbm), (grev_ref, grev_hbm))
        return [pltpu.make_async_copy(a.at[here], b.at[here], out_sem.at[3 * i + k]) for k, (a, b) in enumerate(pairs)]
    for i in range(CH // BLOCKS):
        for copy in fetch(i):
            copy.start()
    whole = ((cot_hbm, cot_ref), (pi_hbm, pi_ref), (pit_hbm, pit_ref), (po_hbm, po_ref), (pot_hbm, pot_ref), (f_hbm, f_ref))
    whole = [pltpu.make_async_copy(a, b, sem.at[i]) for i, (a, b) in enumerate(whole)]
    for copy in whole:
        copy.start()

    unpack_rims(at_ref[0], south_ref, north_ref, fold_ref, mirror_ref, rim, edge)

    def conv_block(i, _):
        for copy in fetch(i):
            copy.wait()
        for j in range(BLOCKS):
            c = i * BLOCKS + j
            t = i * (BLOCKS // 16) + j // 16
            operand(c, j % 16, m_ref[c], side_ref[t], rim[pl.ds(pl.multiple_of(c * 8, 8), 8), :], edge[t], im.at[c])
        for j in range(BLOCKS):
            c = i * BLOCKS + j
            s[pl.ds(pl.multiple_of(c * R, R), R), :] = jnp.dot(t_ref[c][:, :TAPS], im[c], preferred_element_type=F)
        keep(i).start()
        return 0
    lax.fori_loop(0, CH // BLOCKS, conv_block, 0)
    ocean = land_ref[...].astype(F)

    def sum_block(i, acc):
        for j in range(BLOCKS):
            acc = acc + s[pl.ds(pl.multiple_of((i * BLOCKS + j) * R, R), R), :]
        return acc
    mean = lax.fori_loop(0, CH // BLOCKS, sum_block, jnp.zeros((R, Q), F)) * (1.0 / CH)

    def sq_block(i, acc):
        for j in range(BLOCKS):
            d = s[pl.ds(pl.multiple_of((i * BLOCKS + j) * R, R), R), :] - mean
            acc = acc + d * d
        return acc
    var = lax.fori_loop(0, CH // BLOCKS, sq_block, jnp.zeros((R, Q), F)) * (1.0 / CH)
    rstd = lax.rsqrt(var + 1e-6)

    def norm_block(i, _):
        for j in range(BLOCKS):
            c = i * BLOCKS + j
            rows = pl.ds(pl.multiple_of(c * R, R), R)
            s[rows, :] = (s[rows, :] - mean) * rstd
            mcs[rows, :] = cot_ref[c].astype(F) * ocean
        return 0
    whole[0].wait()
    lax.fori_loop(0, CH // BLOCKS, norm_block, 0)
    u[pl.ds(CH * R, R), :] = rstd
    gain = gain_ref[...]
    gacc[...] = jnp.zeros_like(gacc)

    def rows_step(p, _):
        r0 = p * 2
        cells = pl.ds(pl.multiple_of(p * 256, 256), 256)
        nrm = jnp.concatenate([s[pl.ds(r0, CH, stride=R), :], s[pl.ds(r0 + 1, CH, stride=R), :]], axis=1)
        scaled = (nrm * gain).astype(B)
        mc = jnp.concatenate([mcs[pl.ds(r0, CH, stride=R), :], mcs[pl.ds(r0 + 1, CH, stride=R), :]], axis=1).astype(B)
        sc[:, cells] = scaled
        mcb[:, cells] = mc
        mixed = jnp.zeros((CH, 256), F)
        gn = jnp.zeros((CH, 256), F)
        hidden = jnp.dot(pi_ref[...], scaled, preferred_element_type=F)
        grad_act = jnp.dot(pot_ref[...], mc, preferred_element_type=F)
        for h in range(3):
            hs = slice(h * 256, (h + 1) * 256)
            v = hidden[hs]
            ga = grad_act[hs]
            sq = v * v
            t = jnp.tanh(v * (C1 * sq + C0))
            half = 0.5 * t + 0.5
            a = v * half
            d = half + a * (1.0 - half) * (6.0 * C1 * sq + 2.0 * C0)
            ab = a.astype(B)
            gb = (ga * d).astype(B)
            act[hs, cells] = ab
            gh[hs, cells] = gb
            mixed = mixed + jnp.dot(po_ref[:, hs], ab, preferred_element_type=F)
            gn = gn + jnp.dot(pit_ref[:, hs], gb, preferred_element_type=F)
        rs = jnp.concatenate([u[pl.ds(CH * R + r0, 1), :], u[pl.ds(CH * R + r0 + 1, 1), :]], axis=1)
        gnn = gn * nrm
        gacc[...] += gnn[:, :Q] + gnn[:, Q:]
        gs = gn * gain
        m1 = jnp.sum(gs, axis=0, keepdims=True) * (1.0 / CH)
        m2 = jnp.sum(gnn * gain, axis=0, keepdims=True) * (1.0 / CH)
        gcv = rs * (gs - m1 - nrm * m2)
        for h in range(2):
            cut = slice(h * Q, (h + 1) * Q)
            u[pl.ds(r0 + h, CH, stride=R), :] = mixed[:, cut]
            g[pl.ds(r0 + h, CH, stride=R), :] = gcv[:, cut]
            grev[pl.ds(R - 1 - r0 - h, CH, stride=R), :] = gcv[:, cut]
        return 0
    for copy in whole[1:5]:
        copy.wait()
    lax.fori_loop(0, R // 2, rows_step, 0)
    whole[5].wait()

    lane = lanes(R)

    def out_block(i, _):
        held = None
        for j in range(BLOCKS):
            c = i * BLOCKS + j
            rows = pl.ds(pl.multiple_of(c * R, R), R)
            up_ref[c] = (f_ref[c].astype(F) + ocean * u[rows, :]).astype(B)
            gb = g[rows, :].astype(B)
            gc_ref[c] = gb
            grev_ref[c] = grev[rows, :].astype(B)
            held = pack_sides(gb, j % 16, None if j % 16 == 0 else held, lane)
            if j % 16 == 15:
                gside_ref[i * (BLOCKS // 16) + j // 16] = held
        for copy in send(i):
            copy.start()
        return 0
    lax.fori_loop(0, CH // BLOCKS, out_block, 0)
    for k in range(3):
        low_ref[pl.ds(k * CH, CH), :] = g[pl.ds(k, CH, stride=R), :].astype(B)
        high_ref[pl.ds(k * CH, CH), :] = g[pl.ds(R - 3 + k, CH, stride=R), :].astype(B)
    wall[pl.ds(12 * CH, 256), :] = jnp.zeros((256, Q), B)
    for h in range(6):
        hs = slice(h * Q, (h + 1) * Q)
        wall[pl.ds(h * CH, CH), :] = lax.dot_general(mcb[...], act[hs, :], NT, preferred_element_type=F).astype(B)
        wall[pl.ds((6 + h) * CH, CH), :] = lax.dot_general(sc[...], gh[hs, :], NT, preferred_element_type=F).astype(B)
    for i in range(CH // BLOCKS):
        keep(i).wait()
        for copy in send(i):
            copy.wait()


def front(at, masked, side, south, north, fold, t, fields, cot, land, gain, pi, pit, po, pot, after):
    block, rim = jax.ShapeDtypeStruct((CH, R, Q), B), jax.ShapeDtypeStruct((3 * CH, Q), B)
    plane = pltpu.VMEM((CH * R, Q), F)
    return pl.pallas_call(
        front_kernel,
        out_shape=(block, block, block, jax.ShapeDtypeStruct((12, R, Q), B), rim, rim, jax.ShapeDtypeStruct((CH, Q), F),
                   jax.ShapeDtypeStruct((2560, Q), B), jax.ShapeDtypeStruct((CH, TAPS, Q), B)),
        in_specs=[SM, HBM, VM, VM, VM, VM, HBM, HBM, HBM, VM, VM, HBM, HBM, HBM, HBM, VM, HBM], out_specs=(HBM,) * 3 + (VM,) * 5 + (HBM,),
        scratch_shapes=[
            pltpu.VMEM((CH, TAPS, Q), B), pltpu.VMEM((CH * 8, Q), F), pltpu.VMEM((12, 8, Q), F),
            plane, plane, pltpu.VMEM((CH * R + R, Q), F), plane, plane,
            pltpu.VMEM((CH, R * Q), B), pltpu.VMEM((CH, R * Q), B), pltpu.VMEM((HID, R * Q), B), pltpu.VMEM((HID, R * Q), B),
            pltpu.SemaphoreType.DMA((CH // BLOCKS,)),
            pltpu.VMEM((CH, R, Q), B), pltpu.VMEM((CH, R, 256), B), pltpu.VMEM((CH, R, Q), B), pltpu.VMEM((CH, R, Q), B),
            pltpu.VMEM((HID, CH), B), pltpu.VMEM((CH, HID), B), pltpu.VMEM((CH, HID), B), pltpu.VMEM((HID, CH), B),
            pltpu.SemaphoreType.DMA((CH // BLOCKS,)), pltpu.SemaphoreType.DMA((CH // BLOCKS,)), pltpu.SemaphoreType.DMA((6,)),
            pltpu.VMEM((CH, R, Q), B), pltpu.VMEM((CH, R, Q), B), pltpu.VMEM((CH, R, Q), B), pltpu.SemaphoreType.DMA((CH // BLOCKS * 3,)),
        ],
        compiler_params=pltpu.CompilerParams(vmem_limit_bytes=58 << 20),
        cost_estimate=pl.CostEstimate(flops=6 << 30, bytes_accessed=12 << 20, transcendentals=3 << 20),
        name="front",
    )(at, masked, side, south, north, fold, t, fields, cot, land, gain, pi, pit, po, pot, mirrors(), after)


def tap_kernel(im_hbm, grev_hbm, gacc_ref, valid_ref, collect_ref, w_ref, o_ref, im_ref, grev_ref, dks, im_sem, grev_sem):
    def fetch(i):
        here = pl.ds(i * BLOCKS, BLOCKS)
        return (pltpu.make_async_copy(im_hbm.at[here], im_ref.at[here], im_sem.at[i]),
                pltpu.make_async_copy(grev_hbm.at[here], grev_ref.at[here], grev_sem.at[i]))
    for i in range(CH // BLOCKS):
        for copy in fetch(i):
            copy.start()

    def block(i, _):
        for copy in fetch(i):
            copy.wait()
        sums = [[], []]
        for j in range(BLOCKS):
            dt = lax.dot_general(grev_ref[i * BLOCKS + j], im_ref[i * BLOCKS + j], NT, preferred_element_type=F)
            dt = [dt[:, :Q], jnp.concatenate([dt[:, Q:], jnp.zeros((R, 256 - TAPS), F)], axis=1)]
            for h in range(2):
                x = pltpu.roll(dt[h] * valid_ref[:, h * Q:(h + 1) * Q], 0, 1, stride=1, stride_axis=0)
                sums[h].append(jnp.sum(x, axis=0, keepdims=True))
        for h in range(2):
            dks[pl.ds(pl.multiple_of(i * BLOCKS, BLOCKS), BLOCKS), h * Q:(h + 1) * Q] = jnp.concatenate(sums[h], axis=0)
        return 0
    lax.fori_loop(0, CH // BLOCKS, block, 0)
    taps = jnp.dot(dks[...], collect_ref[...], preferred_element_type=F, precision=lax.Precision.HIGHEST)
    gg = jnp.sum(gacc_ref[...], axis=1, keepdims=True)
    o_ref[:CH, :] = jnp.where(lanes(CH) == Q - 1, gg, taps).astype(B)
    o_ref[CH:, :] = jnp.zeros((256 - CH, Q), B)


def taps(kept, grev, gacc, w):
    blocks = CH // BLOCKS
    return pl.pallas_call(
        tap_kernel,
        grid=(1,),
        out_shape=jax.ShapeDtypeStruct(w.shape, B),
        in_specs=[HBM, HBM, VM, VM, VM, HBM],
        out_specs=pl.BlockSpec((256, Q), lambda i: (9, 0)),
        scratch_shapes=[pltpu.VMEM((CH, TAPS, Q), B), pltpu.VMEM((CH, R, Q), B), pltpu.VMEM((CH, 256), F),
                        pltpu.SemaphoreType.DMA((blocks,)), pltpu.SemaphoreType.DMA((blocks,))],
        compiler_params=pltpu.CompilerParams(vmem_limit_bytes=58 << 20),
        cost_estimate=pl.CostEstimate(flops=2 << 30, bytes_accessed=8 << 20, transcendentals=0),
        input_output_aliases={5: 0},
        name="taps",
    )(kept, grev, gacc, jnp.asarray(VALID[::-1].copy()), jnp.asarray(COLLECT), w)


def back_kernel(first, at_ref, m_ref, side_ref, south_ref, north_ref, fold_ref, t_ref, cot_ref, land_ref, mirror_ref, after_ref, *refs):
    o_ref, im, rim, edge = refs[-4:]
    i = pl.program_id(0)

    @pl.when(i == 0)
    def _():
        unpack_rims(at_ref[0], south_ref, north_ref, fold_ref, mirror_ref, rim, edge)
    ocean = land_ref[...].astype(F)
    for j in range(BLOCKS):
        c = (first + i) * BLOCKS + j
        t = (first + i) * (BLOCKS // 16) + j // 16
        operand(c, j % 16, m_ref[j], side_ref[t], rim[pl.ds(pl.multiple_of(c * 8, 8), 8), :], edge[t], im.at[j])
    for j in range(BLOCKS):
        gm = jnp.dot(t_ref[j][:, :TAPS], im[j], preferred_element_type=F)
        o_ref[j] = (cot_ref[j].astype(F) + ocean * gm).astype(B)


def back(at, grad, rims, t, cot, land, after, first, count, begun=None):
    some = lambda *shape: pl.BlockSpec((BLOCKS,) + shape, lambda i: (first + i, 0, 0))
    anywhere = HBM
    extra = [] if begun is None else [begun]
    return pl.pallas_call(
        lambda *refs: back_kernel(first, *refs),
        grid=(count,),
        out_shape=jax.ShapeDtypeStruct((CH, R, Q), B),
        in_specs=[SM, some(R, Q), VM, VM, VM, VM, some(R, 256), some(R, Q), VM, VM, anywhere] + [anywhere] * len(extra),
        out_specs=some(R, Q),
        scratch_shapes=[pltpu.VMEM((BLOCKS, TAPS, Q), B), pltpu.VMEM((CH * 8, Q), F), pltpu.VMEM((12, 8, Q), F)],
        compiler_params=pltpu.CompilerParams(vmem_limit_bytes=56 << 20),
        cost_estimate=pl.CostEstimate(flops=1 << 30, bytes_accessed=8 << 20, transcendentals=0),
        input_output_aliases={11: 0} if extra else {},
        name="back",
    )(at, grad, *rims, t, cot, land, mirrors(), after, *extra)


def half_kernel(at_ref, w_hbm, *refs):
    o_ref, sem = refs[-2:]
    copy = pltpu.make_async_copy(w_hbm.at[pl.ds(pl.multiple_of((1 - at_ref[3]) * 1280, 1280), 1280)], o_ref, sem)
    copy.start()
    copy.wait()


def half(at, w, *after):
    return pl.pallas_call(
        half_kernel, out_shape=jax.ShapeDtypeStruct((1280, Q), B),
        in_specs=[SM, HBM] + [HBM] * len(after), out_specs=VM, name="half",
        scratch_shapes=[pltpu.SemaphoreType.DMA],
        compiler_params=pltpu.CompilerParams(vmem_limit_bytes=8 << 20),
    )(at, w, *after)


def merge_kernel(at_ref, w_hbm, other_ref, after_ref, o_ref, own, sem):
    copy = pltpu.make_async_copy(w_hbm.at[pl.ds(pl.multiple_of(at_ref[3] * 1280, 1280), 1280)], own, sem)
    copy.start()
    copy.wait()
    o_ref[...] = (own[...].astype(F) + other_ref[...].astype(F)).astype(B)


def merge(at, w, other, after):
    return pl.pallas_call(
        merge_kernel, out_shape=jax.ShapeDtypeStruct((1280, Q), B),
        in_specs=[SM, HBM, VM, HBM], out_specs=VM, name="merge",
        scratch_shapes=[pltpu.VMEM((1280, Q), B), pltpu.SemaphoreType.DMA],
        compiler_params=pltpu.CompilerParams(vmem_limit_bytes=8 << 20),
    )(at, w, other, after)


def spread_kernel(x_ref, *refs):
    o_ref = refs[-1]
    total = x_ref[0].astype(F)
    for k in range(1, x_ref.shape[0]):
        total = total + x_ref[k].astype(F)
    total = total.astype(B)
    for k in range(o_ref.shape[0]):
        o_ref[k] = total


def spread(x, copies, *after):
    return pl.pallas_call(
        spread_kernel, out_shape=jax.ShapeDtypeStruct((copies,) + x.shape[1:], B),
        in_specs=[VM] + [HBM] * len(after), out_specs=VM, name="spread",
        compiler_params=pltpu.CompilerParams(vmem_limit_bytes=8 << 20),
    )(x, *after)


def along(i, bits):
    code = (i ^ (i >> 1)) ^ bits
    return code ^ (code >> 1)


def finish_kernel(at_ref, a_ref, b_ref, after_ref, out_ref, in_ref, kern_ref, gain_ref, wall):
    x, y, c = at_ref[1], at_ref[2], at_ref[3]
    for k in range(32):
        src = (a_ref, b_ref)[k // 16]
        chunk = along(x, k % 4) * 4 + along(y, k // 4 % 4) + (c ^ (k // 16)) * 16
        wall[pl.ds(pl.multiple_of(chunk * 80, 80), 80), :] = src[pl.ds(k % 16 * 80, 80), :]
    scale = (128 * 4096) ** -0.5
    for h in range(6):
        hs = slice(h * Q, (h + 1) * Q)
        out_ref[:, hs] = wall[pl.ds(h * CH, CH), :].astype(F) * scale
        in_ref[:, hs] = wall[pl.ds((6 + h) * CH, CH), :].astype(F) * scale
    tail = jnp.transpose(wall[pl.ds(12 * CH, CH), :].astype(F) * scale)
    for a in range(7):
        kern_ref[a] = tail[8 * a:8 * a + 7, :]
    gain_ref[...] = tail[Q - 1:, :]


def finish(at, first, second, after):
    shapes = ((CH, HID), (CH, HID), (7, 7, CH), (1, CH))
    return pl.pallas_call(
        finish_kernel,
        out_shape=tuple(jax.ShapeDtypeStruct(x, F) for x in shapes),
        in_specs=[SM, VM, VM, HBM], out_specs=(VM,) * 4, name="finish",
        scratch_shapes=[pltpu.VMEM((2560, Q), B)],
        compiler_params=pltpu.CompilerParams(vmem_limit_bytes=16 << 20),
    )(at, first, second, after)


ALL = ("x", "yh", "z", "yl", "c")
LAT, LON = 8, 32
PLANE = ("x", "yh", "yl")


def lon_route(step):
    return [(y * LON + i, y * LON + (i + step) % LON) for y in range(LAT) for i in range(LON)]


def rims(side, low, high, after):
    left = lax.ppermute(side, ALL, lon_route(1))
    right = lax.ppermute(side, ALL, lon_route(-1))
    side, low, high = corners(left, right, low, high, after)
    top = LON * (LAT - 1)
    fold = lax.ppermute(high, ALL, [(top + i, top + LON - 1 - i) for i in range(LON)])
    south = lax.ppermute(high, ALL, [(y * LON + i, (y + 1) * LON + i) for y in range(LAT - 1) for i in range(LON)])
    north = lax.ppermute(low, ALL, [(y * LON + i, (y - 1) * LON + i) for y in range(1, LAT) for i in range(LON)])
    return (side, south, north, fold), (left, right)


def swap_route(bx=0, by=0, bc=0):
    def flat(x, y, z, c):
        return ((x * 2 + y // 2) * 8 + z) * 4 + (y % 2) * 2 + c
    return [
        (flat(x, y, z, c), flat(along(x, bx), along(y, by), z, c ^ bc))
        for x in range(4) for y in range(4) for z in range(8) for c in range(2)
    ]


def on_device(fields, cotangent, land_sea, kernel, ln_gain, proj_in, proj_out):
    x, y, c = lax.axis_index("x"), lax.axis_index("yh") * 2 + lax.axis_index("yl"), lax.axis_index("c")
    is_top = x * 2 + lax.axis_index("yh") == LAT - 1
    at = jnp.stack([is_top.astype(jnp.int32), x, y, c]).astype(jnp.int32)
    masked, side, low, high = start(fields, land_sea)
    one, gain = forward_matrices(kernel, ln_gain)
    ends, _ = rims(side, low, high, one)
    two, pi, pot = backward_matrices(at, kernel, proj_in.T, proj_out)
    updated, grad, reverse, side, low, high, gacc, w, kept = front(
        at, masked, *ends, one, fields, cotangent, land_sea, gain, pi, proj_in.T, proj_out, pot, two)
    w = taps(kept, reverse, gacc, w)
    ends, beside = rims(side, low, high, w)
    other = lax.ppermute(half(at, w, *beside), ALL, swap_route(bc=1))
    w = merge(at, w, other, ends[0])
    w = spread(lax.all_to_all(w.reshape(16, 80, Q), PLANE, 0, 0), 8, *ends)
    grad_fields = back(at, grad, ends, two, cotangent, land_sea, w, 0, 6)
    w = spread(lax.all_to_all(w, "z", 0, 0), 1, grad_fields)[0]
    w = jnp.concatenate([w] + [lax.ppermute(w, ALL, swap_route(bx=k)) for k in (1, 2, 3)])
    w = jnp.concatenate([w] + [lax.ppermute(w, ALL, swap_route(by=k)) for k in (1, 2, 3)])
    grad_out, grad_in, grad_kernel, grad_gain = finish(at, w, lax.ppermute(w, ALL, swap_route(bc=1)), grad_fields)
    return updated, grad_fields, grad_kernel.transpose(2, 0, 1), grad_gain.reshape(CH), grad_in.T, grad_out


def solution(mesh):
    fine = jax.sharding.Mesh(mesh.devices.reshape(4, 2, 8, 2, 2), ALL)
    P = jax.sharding.PartitionSpec
    lat, lon = ("x", "yh"), ("z", "yl", "c")
    block = P(None, lat, lon)
    return jax.shard_map(
        on_device,
        mesh=fine,
        in_specs=(block, block, P(lat, lon), P(), P(), P(), P()),
        out_specs=(block, block, P(), P(), P(), P()),
        check_vma=False,
    )
```
